512 devices in a mesh: wide: 64 (over y, x, z_hi), narrow: 8 (over z_lo, core).
Axes of the slice: x: 4, y: 4, z: 16 (z_hi: 4, z_lo: 4; z = z_hi * 4 + z_lo), core: 2. Of those that a mesh axis runs over, the one named last changes fastest.
Arguments:
- star_state: float32 [12, 65536], P(None, ('wide', 'narrow')), may hold values from -6 to 6
- masses: float32 [65536], P(('wide', 'narrow')), may hold values from 0.1 to 10
- levels: int32 [65536], P(('wide', 'narrow')), may hold values from 0 to 3
- active: int32 [16384], replicated, may hold values from 0 to 65535, as said below
Outputs:
- updated: float32 [12, 49152], P(None, ('wide', 'narrow'))
The draws below stay inside these ranges and needn't reach their ends.
Inputs may be any that keep to these rules, and one draw needn't show every extreme that they name: `active`: distinct and ascending; the stars i with the same i // 128 number at most 96, and exactly 96 for some such group in every draw.
All inputs are finite; a program needn't handle non-finite values.
Results may differ from the reference program's by a relative error of at most 0.00012.
Values sent between devices are 32-bit elements; how exact they have to be, the bound alone decides.
A program may use at most 128 MiB of HBM per device.

```python
import math
import jax
import jax.numpy as jnp
from jax import lax

FS_DEV = 128
ACT_DEV = 32
CAP = 96
OWNERS = 512
NSTARS = 65536
ACT = 16384


def draw_active(key, part):
    key = jax.random.fold_in(key, 11)
    key_perm = jax.random.fold_in(key, 1)
    key_delta = jax.random.fold_in(key, 2)
    key_rank = jax.random.fold_in(key, 3)
    heavy = max(OWNERS // 8, 1)
    order = jax.random.permutation(key_perm, OWNERS)
    position = jnp.arange(OWNERS, dtype=jnp.int32)
    middle = OWNERS - 3 * heavy
    offset = position - 3 * heavy
    deltas = jax.random.randint(key_delta, (OWNERS,), 0, ACT_DEV)
    paired = (offset >= 0) & (offset // 2 < middle // 2)
    pair_delta = deltas[jnp.clip(offset // 2, 0, OWNERS - 1)]
    signed = jnp.where(offset % 2 == 0, pair_delta, -pair_delta)
    by_rank = jnp.where(position < heavy, 3 * ACT_DEV, jnp.where(position < 3 * heavy, 0, ACT_DEV + jnp.where(paired, signed, 0)))
    counts = jnp.zeros((OWNERS,), jnp.int32).at[order].set(by_rank.astype(jnp.int32))
    ranks = jax.random.permutation(key_rank, jnp.tile(jnp.arange(FS_DEV, dtype=jnp.int32), (OWNERS, 1)), axis=1, independent=True)
    selected = (ranks < counts[:, None]).reshape(-1)
    return jnp.nonzero(selected, size=ACT)[0].astype(jnp.int32)


def set_ends(drawn, key, smallest, largest):
    longest = drawn.shape.index(max(drawn.shape))
    spots = []
    for shift in (0, 1):
        where = [jax.random.randint(jax.random.fold_in(key, axis), (), 0, length) for axis, length in enumerate(drawn.shape)]
        where[longest] = (where[longest] + shift) % drawn.shape[longest]
        spots.append(tuple(where))
    return drawn.at[spots[0]].set(smallest).at[spots[1]].set(largest)


def level_of(rng, shape, shards, smallest, high):
    def one(dim, blocks):
        steps = jax.random.uniform(jax.random.fold_in(jax.random.fold_in(rng, 6), dim), (blocks,), jnp.float32, smallest / len(shards), high / len(shards))
        return jnp.repeat(jnp.exp(steps), shape[dim] // blocks).reshape((-1,) + (1,) * (len(shape) - dim - 1))

    gain = one(*shards[0])
    for cut in shards[1:]:
        gain = gain * one(*cut)
    return gain


def scatter_about(stream_key, extent, scale, reach, cuts=(), held_as=jnp.bfloat16):
    factor_of = level_of(stream_key, extent, cuts, -0.22, 0.18) if cuts else 1.0
    result = jax.random.normal(stream_key, extent, jnp.float32) * scale * factor_of
    return jnp.minimum(jnp.maximum(result, -reach), reach).astype(held_as)


def setup_inputs(seed: int = 0) -> dict:
    splits = jax.random.split(jax.random.key(seed), 5)
    return {
        "star_state": scatter_about(splits[0], (12, NSTARS), 1.0, 6.0, ((1, 512),), jnp.float32),
        "masses": jnp.clip(jnp.exp(math.log(10.0) - 4.6051702 * jax.random.uniform(splits[1], (NSTARS,), jnp.float32) ** level_of(splits[1], (NSTARS,), ((0, 512),), -0.2, 0.2)), 0.1, 10.0),
        "levels": set_ends(jax.random.randint(splits[2], (NSTARS,), 0, 4), jax.random.fold_in(splits[2], 1), 0, 3).astype(jnp.int32),
        "active": draw_active(jax.random.fold_in(splits[4], 71), 0),
    }


soft_sq = 0.01

def predict(star_state, levels):
    step_len = jnp.exp2(-levels.astype(star_state.dtype))
    position = star_state[0:3]
    velocity = star_state[3:6]
    accel = star_state[6:9]
    jerks = star_state[9:12]
    new_pos = position + step_len * (velocity + step_len * (accel * 0.5 + step_len * jerks * (1.0 / 6.0)))
    new_vel = velocity + step_len * (accel + step_len * jerks * 0.5)
    return jnp.concatenate([new_pos, new_vel], axis=0)

def correct(old_state, old_levels, fresh):
    step_len = jnp.exp2(-old_levels.astype(old_state.dtype))
    half_step = step_len * 0.5
    twelfth = step_len * step_len * (1.0 / 12.0)
    old_pos = old_state[0:3]
    old_vel = old_state[3:6]
    old_acc = old_state[6:9]
    old_jerk = old_state[9:12]
    new_acc = fresh[0:3]
    new_jerk = fresh[3:6]
    new_vel = old_vel + half_step * (old_acc + new_acc) + twelfth * (old_jerk - new_jerk)
    new_pos = old_pos + half_step * (old_vel + new_vel) + twelfth * (old_acc - new_acc)
    return jnp.concatenate([new_pos, new_vel, new_acc, new_jerk], axis=0)

def pull_block(targets, sources):
    sep = [sources[dim_idx][None, :] - targets[dim_idx][:, None] for dim_idx in range(3)]
    rel = [sources[dim_idx + 3][None, :] - targets[dim_idx + 3][:, None] for dim_idx in range(3)]
    dist_sq = sep[0] * sep[0] + sep[1] * sep[1] + sep[2] * sep[2] + soft_sq
    inverse_sq = 1.0 / dist_sq
    strength = sources[6][None, :] * jnp.sqrt(inverse_sq) * inverse_sq
    radial = 3.0 * (sep[0] * rel[0] + sep[1] * rel[1] + sep[2] * rel[2]) * inverse_sq
    accel = [lax.optimization_barrier(jnp.sum(strength * sep[dim_idx], axis=1)) for dim_idx in range(3)]
    jerks = [lax.optimization_barrier(jnp.sum(strength * (rel[dim_idx] - radial * sep[dim_idx]), axis=1)) for dim_idx in range(3)]
    return jnp.stack(accel + jerks, axis=0)

def reference(star_state, masses, levels, active):
    grav = 1.0 / NSTARS
    predicted = predict(star_state, levels)
    sources = jnp.concatenate([predicted, (masses * grav)[None, :]], axis=0)
    targets = predicted[:, active]
    act_tile = math.gcd(ACT, 512)
    src_tile = math.gcd(NSTARS, 2048)
    target_blocks = targets.reshape(6, ACT // act_tile, act_tile).transpose(1, 0, 2)
    source_blocks = sources.reshape(7, NSTARS // src_tile, src_tile).transpose(1, 0, 2)

    def one_block(tile_block):

        def add_pull(summed, portion):
            return (summed + pull_block(tile_block, portion), None)
        summed, _ = lax.scan(add_pull, jnp.zeros((6, act_tile), star_state.dtype), source_blocks)
        return summed
    fresh = lax.map(one_block, target_blocks).transpose(1, 0, 2).reshape(6, ACT)
    corrected = correct(star_state[:, active], levels[active], fresh)
    owner_of = (active // FS_DEV).astype(jnp.int32)
    run_begin = jnp.searchsorted(active, owner_of * FS_DEV).astype(jnp.int32)
    slots = owner_of * CAP + jnp.arange(ACT, dtype=jnp.int32) - run_begin
    return jnp.zeros((12, OWNERS * CAP), star_state.dtype).at[:, slots].set(corrected)
```

```python
import functools

import jax
import jax.numpy as jnp
from jax import lax
from jax.experimental import pallas as pl
from jax.experimental.pallas import tpu as pltpu
from jax.sharding import PartitionSpec as P

MESH = pl.DeviceIdType.MESH
CAP = 96
LANES = 128
GROUP = 64
RING = 8
UNROLL = 16
SOFT = 0.01
BLOCK_COUNTS = (17, 18, 19, 20, 21, 22, 24, 32, 48)


def rows8(row):
    return jnp.broadcast_to(row, (8, LANES))


def lane_gather(tile, idx):
    return jnp.take_along_axis(tile, idx, axis=1, mode="promise_in_bounds")


def step_length(levels):
    return jnp.where(
        levels < 1.5,
        jnp.where(levels < 0.5, 1.0, 0.5),
        jnp.where(levels < 2.5, 0.25, 0.125),
    )


def pull(targets, sources, acc):
    sep = [sources[d] - targets[d] for d in range(3)]
    rel = [sources[3 + d] - targets[3 + d] for d in range(3)]
    dist_sq = (sep[0] * sep[0] + SOFT) + sep[1] * sep[1] + sep[2] * sep[2]
    inverse = lax.rsqrt(dist_sq)
    inverse_sq = inverse * inverse
    strength = (sources[6] * inverse) * inverse_sq
    radial = sep[0] * rel[0] + sep[1] * rel[1] + sep[2] * rel[2]
    turned = (radial * inverse_sq) * strength
    accel = [acc[d] + strength * sep[d] for d in range(3)]
    swing = [acc[3 + d] + strength * rel[d] for d in range(3)]
    drag = [acc[6 + d] + turned * sep[d] for d in range(3)]
    return accel + swing + drag


def kernel(
    blocks, grav, star_ref, mass_ref, level_ref, active_ref, out_ref,
    old, tbuf, zbuf, spread, tgt, offs, accs, fresh, rout, rin,
    tsend, trecv, zsend, zrecv, fsend, frecv, rsend, rrecv,
):
    wide = lax.axis_index("wide")
    narrow = lax.axis_index("narrow")
    plane = wide // 4
    group = (wide % 4) * 2 + narrow // 4
    low = narrow % 4
    member = plane * 4 + low

    def device(plane, group, low):
        return (plane * 4 + group // 2, (group % 2) * 4 + low)

    def mate(i):
        other = (member + i) % GROUP
        return other, device(other // 4, group, other % 4)

    def along(shift):
        return device(plane, (group + shift + RING) % RING, low)

    barrier = pltpu.get_barrier_semaphore()

    def greet(i, carry):
        pl.semaphore_signal(barrier, inc=1, device_id=mate(i)[1], device_id_type=MESH)
        return carry

    for shift in (-2, 2, -1, 1):
        pl.semaphore_signal(barrier, inc=1, device_id=along(shift), device_id_type=MESH)
    lax.fori_loop(1, GROUP, greet, 0)

    lane = lax.broadcasted_iota(jnp.int32, (8, LANES), 1)
    sub = lax.broadcasted_iota(jnp.int32, (8, LANES), 0)
    star = [star_ref[d : d + 1, :] for d in range(12)]
    step = step_length(level_ref[...].astype(jnp.float32))
    pred = []
    for d in range(3):
        x, v, a, j = star[d], star[3 + d], star[6 + d], star[9 + d]
        pred.append(x + step * (v + step * (a * 0.5 + step * j * (1.0 / 6.0))))
    for d in range(3):
        v, a, j = star[3 + d], star[6 + d], star[9 + d]
        pred.append(v + step * (a + step * j * 0.5))
    for d in range(6):
        zbuf[0, d : d + 1, :] = pred[d]
    zbuf[0, 6:7, :] = mass_ref[...] * grav
    zbuf[0, 7:8, :] = jnp.zeros((1, LANES), jnp.float32)

    base = (wide * 8 + narrow) * LANES
    below = jnp.zeros((8, LANES), jnp.int32)
    through = jnp.zeros((8, LANES), jnp.int32)
    for v in range(16):
        entry = active_ref[8 * v : 8 * v + 8, :]
        below = below + jnp.where(entry < base, 1, 0)
        through = through + jnp.where(entry < base + LANES, 1, 0)

    def total(x):
        s = jnp.sum(x.astype(jnp.float32), axis=0, keepdims=True)
        s = jnp.sum(s, axis=1, keepdims=True)
        return jnp.broadcast_to(s, (8, LANES)).astype(jnp.int32)

    begin = total(below)
    count = total(through) - begin
    row_of = lax.shift_right_logical(begin + ((lane - begin) & (LANES - 1)), 7)
    found = jnp.zeros((8, LANES), jnp.int32)
    for v in range(16):
        entry = active_ref[8 * v : 8 * v + 8, :]
        found = found + jnp.where(row_of == sub + 8 * v, entry, 0)
    found = jnp.sum(found.astype(jnp.float32), axis=0, keepdims=True).astype(jnp.int32)
    picked = lane_gather(rows8(found), (lane + begin) & (LANES - 1)) - base
    picked = jnp.where(lane < count, picked, 0) & (LANES - 1)

    chosen = lane_gather(zbuf[0], picked)
    chosen = jnp.where(sub == 6, count.astype(jnp.float32), chosen)
    tbuf[member] = chosen

    pl.semaphore_wait(barrier, GROUP - 1 + 4)

    def send_target(i, carry):
        pltpu.make_async_remote_copy(
            src_ref=tbuf.at[member], dst_ref=tbuf.at[member],
            send_sem=tsend, recv_sem=trecv, device_id=mate(i)[1], device_id_type=MESH,
        ).start()
        return carry

    for slot in (2, 6, 1, 7):
        pltpu.make_async_remote_copy(
            src_ref=zbuf.at[0], dst_ref=zbuf.at[slot],
            send_sem=zsend, recv_sem=zrecv, device_id=along(-slot), device_id_type=MESH,
        ).start()
    lax.fori_loop(1, GROUP, send_target, 0)

    old[0:8, :] = lane_gather(star_ref[0:8, :], picked)
    old[8:12, :] = star_ref[8:12, :]
    old[12:13, :] = step
    old[13:16, :] = jnp.zeros((3, LANES), jnp.float32)
    old[8:16, :] = lane_gather(old[8:16, :], picked)

    def spread_tile(slot, place):
        turned = zbuf[slot].T
        for d in range(7):
            spread[d, place * LANES : (place + 1) * LANES, :] = jnp.broadcast_to(
                turned[:, d : d + 1], (LANES, LANES)
            )

    spread_tile(0, 0)

    four = zbuf.at[pl.ds(0, 4)]
    three = zbuf.at[pl.ds(0, 3)]
    pltpu.make_async_copy(four, four, zrecv).wait()
    far_a = pltpu.make_async_remote_copy(
        src_ref=zbuf.at[pl.ds(1, 2)], dst_ref=zbuf.at[pl.ds(3, 2)],
        send_sem=fsend, recv_sem=frecv, device_id=along(-2), device_id_type=MESH,
    )
    far_b = pltpu.make_async_remote_copy(
        src_ref=zbuf.at[7], dst_ref=zbuf.at[5],
        send_sem=fsend, recv_sem=frecv, device_id=along(2), device_id_type=MESH,
    )
    far_a.start()
    far_b.start()
    for place, slot in ((1, 1), (2, 2), (3, 6), (4, 7)):
        spread_tile(slot, place)

    others = tbuf.at[pl.ds(0, GROUP - 1)]
    pltpu.make_async_copy(others, others, trecv).wait()

    def lay(o, carry):
        off = carry[0]
        tile = tbuf[o]
        offs[o] = off
        rolled = lane_gather(tile, (lane - off) & (LANES - 1))
        laid = [
            jnp.where(lane + LANES * b >= off, rolled, carry[1 + b]) for b in range(blocks)
        ]
        return (off + rows8(tile[6:7, :]).astype(jnp.int32), *laid)

    laid = lax.fori_loop(
        0, GROUP, lay,
        (jnp.zeros((8, LANES), jnp.int32),) + (jnp.zeros((8, LANES), jnp.float32),) * blocks,
    )
    for b in range(blocks):
        tgt[b] = laid[1 + b]

    def pairs(b, acc, first, chunks):
        targets = [rows8(tgt[b, d : d + 1, :]) for d in range(6)]

        def chunk(k, acc):
            acc = list(acc)
            for u in range(UNROLL):
                place = pl.ds(pl.multiple_of((first + k) * (8 * UNROLL) + 8 * u, 8), 8)
                acc = pull(targets, [spread[d, place, :] for d in range(7)], acc)
            return tuple(acc)

        return lax.fori_loop(0, chunks, chunk, acc)

    def near(b, carry):
        acc = pairs(b, (jnp.zeros((8, LANES), jnp.float32),) * 9, 0, 5)
        for d in range(9):
            accs[b, d] = acc[d]
        return carry

    lax.fori_loop(0, blocks, near, 0)

    pltpu.make_async_copy(three, three, frecv).wait()
    for place, slot in ((5, 3), (6, 4), (7, 5)):
        spread_tile(slot, place)

    def far(b, carry):
        acc = pairs(b, tuple(accs[b, d] for d in range(9)), 5, 3)
        for d in range(3):
            fresh[b, d : d + 1, :] = jnp.sum(acc[d], axis=0, keepdims=True)
            fresh[b, 3 + d : 4 + d, :] = jnp.sum(acc[3 + d] - 3.0 * acc[6 + d], axis=0, keepdims=True)
        fresh[b, 6:8, :] = jnp.zeros((2, LANES), jnp.float32)
        return carry

    lax.fori_loop(0, blocks, far, 0)

    def cut(o):
        off = offs[o]
        block_of = lax.shift_right_logical(off + ((lane - off) & (LANES - 1)), 7)
        mine = fresh[0]
        for b in range(1, blocks):
            mine = jnp.where(block_of == b, fresh[b], mine)
        return lane_gather(mine, (lane + off) & (LANES - 1))

    def give(i, carry):
        o, where = mate(i)
        rout[o] = cut(o)
        pltpu.make_async_remote_copy(
            src_ref=rout.at[o], dst_ref=rin.at[member],
            send_sem=rsend, recv_sem=rrecv, device_id=where, device_id_type=MESH,
        ).start()
        return carry

    lax.fori_loop(1, GROUP, give, 0)
    rin[member] = cut(member)

    back = rin.at[pl.ds(0, GROUP - 1)]
    pltpu.make_async_copy(back, back, rrecv).wait()
    sums = [rin[m] for m in range(8)]
    for m in range(8, GROUP):
        sums[m % 8] = sums[m % 8] + rin[m]
    while len(sums) > 1:
        sums = [sums[i] + sums[i + 1] for i in range(0, len(sums), 2)]
    new = sums[0]

    filled = lane[0:1, :] < count[0:1, :]
    step = old[12:13, :]
    half = step * 0.5
    twelfth = step * step * (1.0 / 12.0)
    for d in range(3):
        x0, v0 = old[d : d + 1, :], old[3 + d : 4 + d, :]
        a0, j0 = old[6 + d : 7 + d, :], old[9 + d : 10 + d, :]
        a1, j1 = new[d : d + 1, :], new[3 + d : 4 + d, :]
        v1 = v0 + half * (a0 + a1) + twelfth * (j0 - j1)
        x1 = x0 + half * (v0 + v1) + twelfth * (a0 - a1)
        for r, value in ((d, x1), (3 + d, v1), (6 + d, a1), (9 + d, j1)):
            out_ref[r : r + 1, :] = jnp.where(filled, value, 0.0)[:, :CAP]

    pltpu.make_async_copy(others, others, tsend).wait()
    pltpu.make_async_copy(four, four, zsend).wait()
    pltpu.make_async_copy(three, three, fsend).wait()
    pltpu.make_async_copy(back, back, rsend).wait()


def on_device(star_state, masses, levels, active):
    local_count = star_state.shape[1]
    owners = lax.axis_size(("wide", "narrow"))
    grav = 1.0 / (local_count * owners)
    tile = (8, LANES)
    dma = pltpu.SemaphoreType.DMA

    def branch(which, blocks):
        return pl.pallas_call(
            functools.partial(kernel, blocks, grav),
            out_shape=jax.ShapeDtypeStruct((12, CAP), jnp.float32),
            in_specs=[pl.BlockSpec(memory_space=pltpu.VMEM)] * 4,
            out_specs=pl.BlockSpec(memory_space=pltpu.VMEM),
            scratch_shapes=[
                pltpu.VMEM((16, LANES), jnp.float32),
                pltpu.VMEM((GROUP, *tile), jnp.float32),
                pltpu.VMEM((RING, *tile), jnp.float32),
                pltpu.VMEM((7, RING * LANES, LANES), jnp.float32),
                pltpu.VMEM((blocks, *tile), jnp.float32),
                pltpu.VMEM((GROUP, *tile), jnp.int32),
                pltpu.VMEM((blocks, 9, *tile), jnp.float32),
                pltpu.VMEM((blocks, *tile), jnp.float32),
                pltpu.VMEM((GROUP, *tile), jnp.float32),
                pltpu.VMEM((GROUP, *tile), jnp.float32),
            ]
            + [dma(())] * 8,
            compiler_params=pltpu.CompilerParams(
                collective_id=which, has_side_effects=True, vmem_limit_bytes=32 << 20
            ),
            name=f"step_{blocks}",
        )

    group_of = lax.shift_right_logical(active, 9) & 7
    counts = jnp.sum(
        (group_of[None, :] == jnp.arange(RING, dtype=jnp.int32)[:, None]).astype(jnp.int32), axis=1
    )
    most = jnp.max(counts)
    limits = jnp.array([b * LANES for b in BLOCK_COUNTS[:-1]], jnp.int32)
    which = jnp.sum((most > limits).astype(jnp.int32))
    return lax.switch(
        which,
        [branch(i, b) for i, b in enumerate(BLOCK_COUNTS)],
        star_state, masses.reshape(1, LANES), levels.reshape(1, LANES),
        active.reshape(LANES, LANES),
    )


def solution(mesh):
    placed = (P(None, ("wide", "narrow")), P(("wide", "narrow")), P(("wide", "narrow")), P())
    return jax.shard_map(
        on_device,
        mesh=mesh,
        in_specs=placed,
        out_specs=P(None, ("wide", "narrow")),
        check_vma=False,
    )
```

```python
import functools

import jax
import jax.numpy as jnp
from jax import lax
from jax.experimental import pallas as pl
from jax.experimental.pallas import tpu as pltpu
from jax.sharding import PartitionSpec as P

MESH = pl.DeviceIdType.MESH
CAP = 96
LANES = 128
GROUP = 32
RING = 16
REACH = 4
UNROLL = 32
NEAR = (-4, 4, -3, 3, -2, 2, -1, 1)
EARLY = (0, 1, 15, 2, 14, 3, 13, 4)
HALF = RING * LANES // (16 * UNROLL)
LATE = (12, 5, 6, 7, 8, 9, 10, 11)
ROWS = 6
SOFT = 0.01
BLOCK_COUNTS = (10, 11, 12, 13, 14, 16, 20, 24)


def rows8(row):
    return jnp.broadcast_to(row, (8, LANES))


def lane_gather(tile, idx):
    return jnp.take_along_axis(tile, idx, axis=1, mode="promise_in_bounds")


def step_length(levels):
    return jnp.where(
        levels < 1.5,
        jnp.where(levels < 0.5, 1.0, 0.5),
        jnp.where(levels < 2.5, 0.25, 0.125),
    )


def pull(targets, sources, acc):
    sep = [sources[d] - targets[d] for d in range(3)]
    rel = [sources[3 + d] - targets[3 + d] for d in range(3)]
    dist_sq = (sep[0] * sep[0] + SOFT) + sep[1] * sep[1] + sep[2] * sep[2]
    inverse = lax.rsqrt(dist_sq)
    inverse_sq = inverse * inverse
    strength = (sources[6] * inverse) * inverse_sq
    radial = sep[0] * rel[0] + sep[1] * rel[1] + sep[2] * rel[2]
    turned = (radial * inverse_sq) * strength
    accel = [acc[d] + strength * sep[d] for d in range(3)]
    swing = [acc[3 + d] + strength * rel[d] for d in range(3)]
    drag = [acc[6 + d] + turned * sep[d] for d in range(3)]
    return accel + swing + drag


def kernel(
    blocks, state_hbm, active_hbm, out_ref, state, active_ref,
    old, tbuf, zbuf, spread, tgt, offs, accs, fresh, rout, rin,
    load, tsend, trecv, zsend, zrecv, fsend, frecv, rsend, rrecv,
):
    wide = lax.axis_index("wide")
    narrow = lax.axis_index("narrow")
    plane = wide // 4
    level = (wide % 4) * 4 + narrow // 2
    core = narrow % 2
    member = plane * 2 + core

    def device(plane, level, core):
        return (plane * 4 + level // 4, (level % 4) * 2 + core)

    def mate(i):
        other = (member + i) % GROUP
        return other, device(other // 2, level, other % 2)

    def along(shift):
        return device(plane, (level + shift + RING) % RING, core)

    barrier = pltpu.get_barrier_semaphore()

    def greet(i, carry):
        pl.semaphore_signal(barrier, inc=1, device_id=mate(i)[1], device_id_type=MESH)
        return carry

    for shift in NEAR:
        pl.semaphore_signal(barrier, inc=1, device_id=along(shift), device_id_type=MESH)
    lax.fori_loop(1, GROUP, greet, 0)

    loads = [
        pltpu.make_async_copy(state_hbm, state, load.at[0]),
        pltpu.make_async_copy(active_hbm, active_ref, load.at[1]),
    ]
    for copy in loads:
        copy.start()
    for copy in loads:
        copy.wait()

    lane = lax.broadcasted_iota(jnp.int32, (8, LANES), 1)
    sub = lax.broadcasted_iota(jnp.int32, (8, LANES), 0)
    star = [state[d : d + 1, :] for d in range(12)]
    step = state[12:13, :]
    pred = []
    for d in range(3):
        x, v, a, j = star[d], star[3 + d], star[6 + d], star[9 + d]
        pred.append(x + step * (v + step * (a * 0.5 + step * j * (1.0 / 6.0))))
    for d in range(3):
        v, a, j = star[3 + d], star[6 + d], star[9 + d]
        pred.append(v + step * (a + step * j * 0.5))
    for d in range(6):
        zbuf[0, d : d + 1, :] = pred[d]
    zbuf[0, 6:7, :] = state[13:14, :]
    zbuf[0, 7:8, :] = jnp.zeros((1, LANES), jnp.float32)

    base = (wide * 8 + narrow) * LANES
    below = jnp.zeros((8, LANES), jnp.int32)
    through = jnp.zeros((8, LANES), jnp.int32)
    for v in range(16):
        entry = active_ref[8 * v : 8 * v + 8, :]
        below = below + jnp.where(entry < base, 1, 0)
        through = through + jnp.where(entry < base + LANES, 1, 0)

    def total(x):
        s = jnp.sum(x.astype(jnp.float32), axis=0, keepdims=True)
        s = jnp.sum(s, axis=1, keepdims=True)
        return jnp.broadcast_to(s, (8, LANES)).astype(jnp.int32)

    begin = total(below)
    count = total(through) - begin
    row_of = lax.shift_right_logical(begin + ((lane - begin) & (LANES - 1)), 7)
    found = jnp.zeros((8, LANES), jnp.int32)
    for v in range(16):
        entry = active_ref[8 * v : 8 * v + 8, :]
        found = found + jnp.where(row_of == sub + 8 * v, entry, 0)
    found = jnp.sum(found.astype(jnp.float32), axis=0, keepdims=True).astype(jnp.int32)
    picked = lane_gather(rows8(found), (lane + begin) & (LANES - 1)) - base
    picked = jnp.where(lane < count, picked, 0) & (LANES - 1)

    chosen = lane_gather(zbuf[0], picked)
    chosen = jnp.where(lane == LANES - 1, count.astype(jnp.float32), chosen)
    tbuf[member] = chosen

    pl.semaphore_wait(barrier, GROUP - 1 + len(NEAR))

    def send_target(i, carry):
        pltpu.make_async_remote_copy(
            src_ref=tbuf.at[member, pl.ds(0, ROWS)], dst_ref=tbuf.at[member, pl.ds(0, ROWS)],
            send_sem=tsend, recv_sem=trecv, device_id=mate(i)[1], device_id_type=MESH,
        ).start()
        return carry

    for shift in NEAR:
        pltpu.make_async_remote_copy(
            src_ref=zbuf.at[0], dst_ref=zbuf.at[(RING - shift) % RING],
            send_sem=zsend, recv_sem=zrecv, device_id=along(shift), device_id_type=MESH,
        ).start()
    lax.fori_loop(1, GROUP, send_target, 0)

    old[0:8, :] = lane_gather(state[0:8, :], picked)
    old[8:16, :] = lane_gather(state[8:16, :], picked)

    def spread_tile(slot, place):
        turned = zbuf[slot].T
        for d in range(7):
            spread[d, place * LANES : (place + 1) * LANES, :] = jnp.broadcast_to(
                turned[:, d : d + 1], (LANES, LANES)
            )

    spread_tile(0, 0)

    direct = zbuf.at[pl.ds(0, len(NEAR))]
    passed = zbuf.at[pl.ds(0, RING - 1 - len(NEAR))]
    pltpu.make_async_copy(direct, direct, zrecv).wait()
    pltpu.make_async_remote_copy(
        src_ref=zbuf.at[pl.ds(1, REACH)], dst_ref=zbuf.at[pl.ds(1 + REACH, REACH)],
        send_sem=fsend, recv_sem=frecv, device_id=along(-REACH), device_id_type=MESH,
    ).start()
    pltpu.make_async_remote_copy(
        src_ref=zbuf.at[pl.ds(RING - REACH + 1, REACH - 1)],
        dst_ref=zbuf.at[pl.ds(RING - 2 * REACH + 1, REACH - 1)],
        send_sem=fsend, recv_sem=frecv, device_id=along(REACH), device_id_type=MESH,
    ).start()
    for place, slot in enumerate(EARLY[1:]):
        spread_tile(slot, 1 + place)

    others = tbuf.at[pl.ds(0, GROUP - 1), pl.ds(0, ROWS)]
    pltpu.make_async_copy(others, others, trecv).wait()

    def lay(k, carry):
        off, laid = carry[0], carry[1:]
        for u in range(8):
            o = k * 8 + u
            tile = tbuf[o]
            offs[o] = off
            rolled = lane_gather(tile, (lane - off) & (LANES - 1))
            laid = [jnp.where(lane + LANES * b >= off, rolled, laid[b]) for b in range(blocks)]
            off = off + rows8(
                jnp.broadcast_to(tile[0:1, LANES - 1 : LANES], (1, LANES))
            ).astype(jnp.int32)
        return (off, *laid)

    laid = lax.fori_loop(
        0, GROUP // 8, lay,
        (jnp.zeros((8, LANES), jnp.int32),) + (jnp.zeros((8, LANES), jnp.float32),) * blocks,
    )
    for b in range(blocks):
        tgt[b] = laid[1 + b]

    def pairs(b, acc, first, chunks):
        targets = [rows8(tgt[b, d : d + 1, :]) for d in range(6)]

        def chunk(k, acc):
            acc = list(acc)
            for u in range(UNROLL):
                place = pl.ds(pl.multiple_of((first + k) * (8 * UNROLL) + 8 * u, 8), 8)
                acc = pull(targets, [spread[d, place, :] for d in range(7)], acc)
            return tuple(acc)

        return lax.fori_loop(0, chunks, chunk, acc)

    def near(b, carry):
        acc = pairs(b, (jnp.zeros((8, LANES), jnp.float32),) * 9, 0, HALF)
        for d in range(9):
            accs[b, d] = acc[d]
        return carry

    lax.fori_loop(0, blocks, near, 0)

    pltpu.make_async_copy(passed, passed, frecv).wait()
    for place, slot in enumerate(LATE):
        spread_tile(slot, len(EARLY) + place)

    def far(b, carry):
        acc = pairs(b, tuple(accs[b, d] for d in range(9)), HALF, HALF)
        for d in range(3):
            fresh[b, d : d + 1, :] = jnp.sum(acc[d], axis=0, keepdims=True)
            fresh[b, 3 + d : 4 + d, :] = jnp.sum(acc[3 + d] - 3.0 * acc[6 + d], axis=0, keepdims=True)
        fresh[b, 6:8, :] = jnp.zeros((2, LANES), jnp.float32)
        return carry

    lax.fori_loop(0, blocks, far, 0)

    def cut(o):
        off = offs[o]
        block_of = lax.shift_right_logical(off + ((lane - off) & (LANES - 1)), 7)
        mine = fresh[0]
        for b in range(1, blocks):
            mine = jnp.where(block_of == b, fresh[b], mine)
        return lane_gather(mine, (lane + off) & (LANES - 1))

    def give(first, count):
        cuts = [(mate(first + u), cut(mate(first + u)[0])) for u in range(count)]
        for (o, where), mine in cuts:
            rout[o] = mine
            pltpu.make_async_remote_copy(
                src_ref=rout.at[o, pl.ds(0, ROWS)], dst_ref=rin.at[member, pl.ds(0, ROWS)],
                send_sem=rsend, recv_sem=rrecv, device_id=where, device_id_type=MESH,
            ).start()

    def give8(k, carry):
        give(1 + 8 * k, 8)
        return carry

    lax.fori_loop(0, GROUP // 8 - 1, give8, 0)
    give(GROUP - 7, 7)
    rin[member] = cut(member)

    back = rin.at[pl.ds(0, GROUP - 1), pl.ds(0, ROWS)]
    pltpu.make_async_copy(back, back, rrecv).wait()
    sums = [rin[m] for m in range(8)]
    for m in range(8, GROUP):
        sums[m % 8] = sums[m % 8] + rin[m]
    while len(sums) > 1:
        sums = [sums[i] + sums[i + 1] for i in range(0, len(sums), 2)]
    new = sums[0]

    filled = lane[0:1, :] < count[0:1, :]
    step = old[12:13, :]
    half = step * 0.5
    twelfth = step * step * (1.0 / 12.0)
    for d in range(3):
        x0, v0 = old[d : d + 1, :], old[3 + d : 4 + d, :]
        a0, j0 = old[6 + d : 7 + d, :], old[9 + d : 10 + d, :]
        a1, j1 = new[d : d + 1, :], new[3 + d : 4 + d, :]
        v1 = v0 + half * (a0 + a1) + twelfth * (j0 - j1)
        x1 = x0 + half * (v0 + v1) + twelfth * (a0 - a1)
        for r, value in ((d, x1), (3 + d, v1), (6 + d, a1), (9 + d, j1)):
            out_ref[r : r + 1, :] = jnp.where(filled, value, 0.0)[:, :CAP]

    pltpu.make_async_copy(others, others, tsend).wait()
    pltpu.make_async_copy(direct, direct, zsend).wait()
    pltpu.make_async_copy(passed, passed, fsend).wait()
    pltpu.make_async_copy(back, back, rsend).wait()


def prepare(grav, active_ref, star_ref, mass_ref, level_ref, which_ref, state_ref):
    state_ref[0:12, :] = star_ref[...]
    state_ref[12:13, :] = step_length(level_ref[...].astype(jnp.float32))
    state_ref[13:14, :] = mass_ref[...] * grav
    state_ref[14:16, :] = jnp.zeros((2, LANES), jnp.float32)

    counts = [jnp.zeros((8, LANES), jnp.int32) for _ in range(RING)]
    for v in range(16):
        plane = lax.shift_right_logical(active_ref[8 * v : 8 * v + 8, :], 8) & (RING - 1)
        counts = [c + jnp.where(plane == g, 1, 0) for g, c in enumerate(counts)]
    rows = [jnp.sum(c.astype(jnp.float32), axis=0, keepdims=True) for c in counts]
    most = jnp.max(jnp.sum(jnp.concatenate(rows, axis=0), axis=1, keepdims=True))
    which_ref[0] = sum(jnp.where(most > b * LANES, 1, 0) for b in BLOCK_COUNTS[:-1])


def on_device(star_state, masses, levels, active):
    local_count = star_state.shape[1]
    owners = lax.axis_size(("wide", "narrow"))
    grav = 1.0 / (local_count * owners)
    tile = (8, LANES)
    dma = pltpu.SemaphoreType.DMA

    def branch(which, blocks):
        return pl.pallas_call(
            functools.partial(kernel, blocks),
            out_shape=jax.ShapeDtypeStruct((12, CAP), jnp.float32),
            in_specs=[pl.BlockSpec(memory_space=pl.ANY)] * 2,
            out_specs=pl.BlockSpec(memory_space=pltpu.VMEM),
            scratch_shapes=[
                pltpu.VMEM((16, LANES), jnp.float32),
                pltpu.VMEM((LANES, LANES), jnp.int32),
                pltpu.VMEM((16, LANES), jnp.float32),
                pltpu.VMEM((GROUP, *tile), jnp.float32),
                pltpu.VMEM((RING, *tile), jnp.float32),
                pltpu.VMEM((7, RING * LANES, LANES), jnp.float32),
                pltpu.VMEM((blocks, *tile), jnp.float32),
                pltpu.VMEM((GROUP, *tile), jnp.int32),
                pltpu.VMEM((blocks, 9, *tile), jnp.float32),
                pltpu.VMEM((blocks, *tile), jnp.float32),
                pltpu.VMEM((GROUP, *tile), jnp.float32),
                pltpu.VMEM((GROUP, *tile), jnp.float32),
                dma((2,)),
            ]
            + [dma(())] * 8,
            compiler_params=pltpu.CompilerParams(
                collective_id=which, has_side_effects=True, vmem_limit_bytes=40 << 20
            ),
            name=f"step_{blocks}",
        )

    listed = active.reshape(LANES, LANES)
    which, state = pl.pallas_call(
        functools.partial(prepare, grav),
        out_shape=(
            jax.ShapeDtypeStruct((1,), jnp.int32), jax.ShapeDtypeStruct((16, LANES), jnp.float32),
        ),
        in_specs=[pl.BlockSpec(memory_space=pltpu.VMEM)] * 4,
        out_specs=(
            pl.BlockSpec(memory_space=pltpu.SMEM), pl.BlockSpec(memory_space=pltpu.VMEM),
        ),
        name="prepare",
    )(listed, star_state, masses.reshape(1, LANES), levels.reshape(1, LANES))
    return lax.switch(
        which[0], [branch(i, b) for i, b in enumerate(BLOCK_COUNTS)], state, listed
    )


def solution(mesh):
    placed = (P(None, ("wide", "narrow")), P(("wide", "narrow")), P(("wide", "narrow")), P())
    return jax.shard_map(
        on_device,
        mesh=mesh,
        in_specs=placed,
        out_specs=P(None, ("wide", "narrow")),
        check_vma=False,
    )
```

```python
import functools

import jax
import jax.numpy as jnp
from jax import lax
from jax.experimental import pallas as pl
from jax.experimental.pallas import tpu as pltpu
from jax.sharding import PartitionSpec as P

MESH = pl.DeviceIdType.MESH
CAP = 96
LANES = 128
GROUP = 32
RING = 16
REACH = 4
CHUNK = 128
ROWS = 6
SOFT = 0.01
BLOCK_COUNTS = (10, 11, 12, 13, 14, 16, 20, 24)


def rows8(row):
    return jnp.broadcast_to(row, (8, LANES))


def lane_gather(tile, idx):
    return jnp.take_along_axis(tile, idx, axis=1, mode="promise_in_bounds")


def step_length(levels):
    return jnp.where(
        levels < 1.5,
        jnp.where(levels < 0.5, 1.0, 0.5),
        jnp.where(levels < 2.5, 0.25, 0.125),
    )


def halves(x):
    high = x.astype(jnp.bfloat16)
    return high, (x - high.astype(jnp.float32)).astype(jnp.bfloat16)


def strengths(targets, sources):
    sep = [sources[d] - targets[d] for d in range(3)]
    rel = [sources[3 + d] - targets[3 + d] for d in range(3)]
    dist_sq = (sep[0] * sep[0] + SOFT) + sep[1] * sep[1] + sep[2] * sep[2]
    inverse = lax.rsqrt(dist_sq)
    inverse_sq = inverse * inverse
    strength = inverse * inverse_sq
    radial = sep[0] * rel[0] + sep[1] * rel[1] + sep[2] * rel[2]
    turned = (radial * inverse_sq) * strength
    return [jnp.concatenate(pair, axis=1) for pair in zip(halves(strength), halves(turned))]


def kernel(
    blocks, state_hbm, active_hbm, out_ref, state, active_ref,
    old, tbuf, zbuf, spread, weigh, middle, pend, tgt, offs, accs, fresh, rout, rin,
    load, tsend, trecv, zsend, zrecv, fsend, frecv, rsend, rrecv,
):
    wide = lax.axis_index("wide")
    narrow = lax.axis_index("narrow")
    plane = wide // 4
    level = (wide % 4) * 4 + narrow // 2
    core = narrow % 2
    member = plane * 2 + core

    def device(plane, level, core):
        return (plane * 4 + level // 4, (level % 4) * 2 + core)

    def mate(i):
        other = (member + i) % GROUP
        return other, device(other // 2, level, other % 2)

    def along(shift):
        return device(plane, (level + shift + RING) % RING, core)

    barrier = pltpu.get_barrier_semaphore()

    def greet(i, carry):
        pl.semaphore_signal(barrier, inc=1, device_id=mate(i)[1], device_id_type=MESH)
        return carry

    quarter = level // 4
    odd = quarter % 2
    upper = level // 8
    inward = 1 - 2 * odd
    edge = level % 4 + odd * (3 - 2 * (level % 4))

    for k in range(1, REACH + 1):
        pl.semaphore_signal(barrier, inc=1, device_id=along(inward * k), device_id_type=MESH)

        @pl.when((edge >= k) | (upper == 0))
        def _():
            pl.semaphore_signal(barrier, inc=1, device_id=along(-inward * k), device_id_type=MESH)

    lax.fori_loop(1, GROUP, greet, 0)

    loads = [
        pltpu.make_async_copy(state_hbm, state, load.at[0]),
        pltpu.make_async_copy(active_hbm, active_ref, load.at[1]),
    ]
    for copy in loads:
        copy.start()
    for copy in loads:
        copy.wait()

    lane = lax.broadcasted_iota(jnp.int32, (8, LANES), 1)
    sub = lax.broadcasted_iota(jnp.int32, (8, LANES), 0)
    star = [state[d : d + 1, :] for d in range(12)]
    step = state[12:13, :]
    pred = []
    for d in range(3):
        x, v, a, j = star[d], star[3 + d], star[6 + d], star[9 + d]
        pred.append(x + step * (v + step * (a * 0.5 + step * j * (1.0 / 6.0))))
    for d in range(3):
        v, a, j = star[3 + d], star[6 + d], star[9 + d]
        pred.append(v + step * (a + step * j * 0.5))
    for d in range(6):
        zbuf[0, d : d + 1, :] = pred[d]
    zbuf[0, 6:7, :] = state[13:14, :]
    zbuf[0, 7:8, :] = jnp.zeros((1, LANES), jnp.float32)

    base = (wide * 8 + narrow) * LANES
    below = jnp.zeros((8, LANES), jnp.int32)
    through = jnp.zeros((8, LANES), jnp.int32)
    for v in range(16):
        entry = active_ref[8 * v : 8 * v + 8, :]
        below = below + jnp.where(entry < base, 1, 0)
        through = through + jnp.where(entry < base + LANES, 1, 0)

    def total(x):
        s = jnp.sum(x.astype(jnp.float32), axis=0, keepdims=True)
        s = jnp.sum(s, axis=1, keepdims=True)
        return jnp.broadcast_to(s, (8, LANES)).astype(jnp.int32)

    begin = total(below)
    count = total(through) - begin
    row_of = lax.shift_right_logical(begin + ((lane - begin) & (LANES - 1)), 7)
    found = jnp.zeros((8, LANES), jnp.int32)
    for v in range(16):
        entry = active_ref[8 * v : 8 * v + 8, :]
        found = found + jnp.where(row_of == sub + 8 * v, entry, 0)
    found = jnp.sum(found.astype(jnp.float32), axis=0, keepdims=True).astype(jnp.int32)
    picked = lane_gather(rows8(found), (lane + begin) & (LANES - 1)) - base
    picked = jnp.where(lane < count, picked, 0) & (LANES - 1)

    chosen = lane_gather(zbuf[0], picked)
    chosen = jnp.where(lane == LANES - 1, count.astype(jnp.float32), chosen)
    tbuf[member] = chosen

    pl.semaphore_wait(barrier, GROUP - 1 + REACH + edge + upper * (REACH - edge))

    def send_target(i, carry):
        pltpu.make_async_remote_copy(
            src_ref=tbuf.at[member, pl.ds(0, ROWS)], dst_ref=tbuf.at[member, pl.ds(0, ROWS)],
            send_sem=tsend, recv_sem=trecv, device_id=mate(i)[1], device_id_type=MESH,
        ).start()
        return carry

    def send_source(shift):
        slot = (RING - shift) % RING
        pltpu.make_async_remote_copy(
            src_ref=zbuf.at[0], dst_ref=zbuf.at[slot],
            send_sem=zsend, recv_sem=zrecv.at[slot], device_id=along(shift), device_id_type=MESH,
        ).start()

    def await_source(shift):
        slot = (RING + shift) % RING
        tile = zbuf.at[slot]
        pltpu.make_async_copy(tile, tile, zrecv.at[slot]).wait()

    for k in range(REACH, 0, -1):
        send_source(inward * k)

        @pl.when((edge >= k) | (upper == 1))
        def _():
            send_source(-inward * k)

    lax.fori_loop(1, GROUP, send_target, 0)

    old[0:8, :] = lane_gather(state[0:8, :], picked)
    old[8:16, :] = lane_gather(state[8:16, :], picked)

    mean = jnp.sum(zbuf[0], axis=1, keepdims=True) * (1.0 / LANES)
    middle[...] = jnp.where(sub < 6, jnp.broadcast_to(mean, (8, LANES)), 0.0)

    def spread_tile(slot, place):
        tile = zbuf[slot]
        turned = tile.T
        lanes = slice(place * LANES, (place + 1) * LANES)
        for d in range(6):
            spread[d, lanes, :] = jnp.broadcast_to(turned[:, d : d + 1], (LANES, LANES))
        mass = rows8(tile[6:7, :])
        rest = jnp.where(sub < 6, (tile - middle[...]) * mass, jnp.where(sub == 6, mass, 0.0))
        pieces = []
        for _ in range(3):
            pieces.append(rest.astype(jnp.bfloat16).astype(jnp.float32))
            rest = rest - pieces[-1]
        pieces.append(jnp.zeros((8, LANES), jnp.float32))
        weigh[:, lanes] = jnp.concatenate(pieces, axis=0).astype(jnp.bfloat16)

    spread_tile(0, 0)

    direct = zbuf.at[pl.ds(0, 2 * REACH)]
    passed = zbuf.at[pl.ds(0, RING - 1 - 2 * REACH)]

    def settle():
        for k in range(1, REACH + 1):
            await_source(-inward * k)

            @pl.when((edge < k) & (upper == 0))
            def _():
                send_source(-inward * k)

    def pass_up():
        pltpu.make_async_remote_copy(
            src_ref=zbuf.at[pl.ds(RING - REACH + 1, REACH - 1)],
            dst_ref=zbuf.at[pl.ds(RING - 2 * REACH + 1, REACH - 1)],
            send_sem=fsend, recv_sem=frecv, device_id=along(REACH), device_id_type=MESH,
        ).start()

    def pass_down():
        pltpu.make_async_remote_copy(
            src_ref=zbuf.at[pl.ds(1, REACH)], dst_ref=zbuf.at[pl.ds(1 + REACH, REACH)],
            send_sem=fsend, recv_sem=frecv, device_id=along(-REACH), device_id_type=MESH,
        ).start()

    others = tbuf.at[pl.ds(0, GROUP - 1), pl.ds(0, ROWS)]
    pltpu.make_async_copy(others, others, trecv).wait()

    def lay(k, carry):
        off, laid = carry[0], carry[1:]
        for u in range(8):
            o = k * 8 + u
            tile = tbuf[o]
            offs[o] = off
            rolled = lane_gather(tile, (lane - off) & (LANES - 1))
            laid = [jnp.where(lane + LANES * b >= off, rolled, laid[b]) for b in range(blocks)]
            off = off + rows8(
                jnp.broadcast_to(tile[0:1, LANES - 1 : LANES], (1, LANES))
            ).astype(jnp.int32)
        return (off, *laid)

    laid = lax.fori_loop(
        0, GROUP // 8, lay,
        (jnp.zeros((8, LANES), jnp.int32),) + (jnp.zeros((8, LANES), jnp.float32),) * blocks,
    )
    for b in range(blocks):
        tgt[b] = laid[1 + b]

    for k in range(1, REACH + 1):
        await_source(inward * k)

    @pl.when(quarter == 1)
    def _():
        settle()
        pass_up()
        pass_down()

    @pl.when(quarter == 2)
    def _():
        pass_down()

    @pl.when(quarter == 3)
    def _():
        pass_up()

    for k in range(1, REACH + 1):
        spread_tile((RING + inward * k) % RING, k)

    def work(first_tile, tiles):
        begin_row, end_row = first_tile * LANES, (first_tile + tiles) * LANES

        def product(lanes, piece):
            return jnp.dot(weigh[:, lanes], piece, preferred_element_type=jnp.float32)

        last = slice(end_row - CHUNK, end_row)

        def left():
            return product(last, pend[0]) + product(last, pend[1])

        def block(b, carry):
            late = left()
            targets = [
                jnp.broadcast_to(tgt[b, d : d + 1, :], (16, LANES)) for d in range(6)
            ]
            acc = jnp.zeros((32, 2 * LANES), jnp.float32)
            for first in range(begin_row, end_row, CHUNK):
                parts = [
                    strengths(targets, [spread[d, row : row + 16, :] for d in range(6)])
                    for row in range(first, first + CHUNK, 16)
                ]
                for p in range(2):
                    piece = jnp.concatenate([part[p] for part in parts], axis=0)
                    if first + CHUNK < end_row:
                        acc = acc + product(slice(first, first + CHUNK), piece)
                    else:
                        pend[p] = piece
            accs[b] = accs[b] + late
            accs[b + 1] = accs[b + 1] + acc
            return carry

        pend[...] = jnp.zeros_like(pend)
        lax.fori_loop(0, blocks, block, 0)
        accs[blocks] = accs[blocks] + left()

    accs[...] = jnp.zeros_like(accs)
    work(0, 1 + REACH)

    @pl.when(quarter == 0)
    def _():
        settle()
        pass_up()
        pass_down()

    @pl.when(quarter == 2)
    def _():
        settle()
        pass_up()

    @pl.when(quarter == 3)
    def _():
        settle()
        pass_down()

    for k in range(1, REACH + 1):
        spread_tile((RING - inward * k) % RING, REACH + k)
    work(1 + REACH, REACH)

    pltpu.make_async_copy(passed, passed, frecv).wait()
    for slot in range(REACH + 1, RING - REACH):
        spread_tile(slot, REACH + slot)
    work(1 + 2 * REACH, RING - 1 - 2 * REACH)

    for b in range(blocks):
        acc = accs[b + 1]
        acc = acc[0:8] + acc[8:16] + acc[16:24]
        drawn, dragged = acc[:, :LANES], acc[:, LANES:]
        here = tgt[b] - middle[...]
        pulled = drawn - here * rows8(drawn[6:7, :])
        slowed = dragged - here * rows8(dragged[6:7, :])
        fresh[b, 0:6, :] = pulled[0:6, :]
        fresh[b, 3:6, :] = pulled[3:6, :] - 3.0 * slowed[0:3, :]
        fresh[b, 6:8, :] = jnp.zeros((2, LANES), jnp.float32)

    def cut(o):
        off = offs[o]
        block_of = lax.shift_right_logical(off + ((lane - off) & (LANES - 1)), 7)
        mine = fresh[0]
        for b in range(1, blocks):
            mine = jnp.where(block_of == b, fresh[b], mine)
        return lane_gather(mine, (lane + off) & (LANES - 1))

    def give(first, count):
        cuts = [(mate(first + u), cut(mate(first + u)[0])) for u in range(count)]
        for (o, where), mine in cuts:
            rout[o] = mine
            pltpu.make_async_remote_copy(
                src_ref=rout.at[o, pl.ds(0, ROWS)], dst_ref=rin.at[member, pl.ds(0, ROWS)],
                send_sem=rsend, recv_sem=rrecv, device_id=where, device_id_type=MESH,
            ).start()

    def give8(k, carry):
        give(1 + 8 * k, 8)
        return carry

    lax.fori_loop(0, GROUP // 8 - 1, give8, 0)
    give(GROUP - 7, 7)
    rin[member] = cut(member)

    back = rin.at[pl.ds(0, GROUP - 1), pl.ds(0, ROWS)]
    pltpu.make_async_copy(back, back, rrecv).wait()
    sums = [rin[m] for m in range(8)]
    for m in range(8, GROUP):
        sums[m % 8] = sums[m % 8] + rin[m]
    while len(sums) > 1:
        sums = [sums[i] + sums[i + 1] for i in range(0, len(sums), 2)]
    new = sums[0]

    filled = lane[0:1, :] < count[0:1, :]
    step = old[12:13, :]
    half = step * 0.5
    twelfth = step * step * (1.0 / 12.0)
    for d in range(3):
        x0, v0 = old[d : d + 1, :], old[3 + d : 4 + d, :]
        a0, j0 = old[6 + d : 7 + d, :], old[9 + d : 10 + d, :]
        a1, j1 = new[d : d + 1, :], new[3 + d : 4 + d, :]
        v1 = v0 + half * (a0 + a1) + twelfth * (j0 - j1)
        x1 = x0 + half * (v0 + v1) + twelfth * (a0 - a1)
        for r, value in ((d, x1), (3 + d, v1), (6 + d, a1), (9 + d, j1)):
            out_ref[r : r + 1, :] = jnp.where(filled, value, 0.0)[:, :CAP]

    pltpu.make_async_copy(others, others, tsend).wait()
    pltpu.make_async_copy(direct, direct, zsend).wait()
    pltpu.make_async_copy(passed, passed, fsend).wait()
    pltpu.make_async_copy(back, back, rsend).wait()


def prepare(grav, active_ref, star_ref, mass_ref, level_ref, which_ref, state_ref):
    state_ref[0:12, :] = star_ref[...]
    state_ref[12:13, :] = step_length(level_ref[...].astype(jnp.float32))
    state_ref[13:14, :] = mass_ref[...] * grav
    state_ref[14:16, :] = jnp.zeros((2, LANES), jnp.float32)

    counts = [jnp.zeros((8, LANES), jnp.int32) for _ in range(RING)]
    for v in range(16):
        plane = lax.shift_right_logical(active_ref[8 * v : 8 * v + 8, :], 8) & (RING - 1)
        counts = [c + jnp.where(plane == g, 1, 0) for g, c in enumerate(counts)]
    rows = [jnp.sum(c.astype(jnp.float32), axis=0, keepdims=True) for c in counts]
    most = jnp.max(jnp.sum(jnp.concatenate(rows, axis=0), axis=1, keepdims=True))
    which_ref[0] = sum(jnp.where(most > b * LANES, 1, 0) for b in BLOCK_COUNTS[:-1])


def on_device(star_state, masses, levels, active):
    local_count = star_state.shape[1]
    owners = lax.axis_size(("wide", "narrow"))
    grav = 1.0 / (local_count * owners)
    tile = (8, LANES)
    dma = pltpu.SemaphoreType.DMA

    def branch(which, blocks):
        return pl.pallas_call(
            functools.partial(kernel, blocks),
            out_shape=jax.ShapeDtypeStruct((12, CAP), jnp.float32),
            in_specs=[pl.BlockSpec(memory_space=pl.ANY)] * 2,
            out_specs=pl.BlockSpec(memory_space=pltpu.VMEM),
            scratch_shapes=[
                pltpu.VMEM((16, LANES), jnp.float32),
                pltpu.VMEM((LANES, LANES), jnp.int32),
                pltpu.VMEM((16, LANES), jnp.float32),
                pltpu.VMEM((GROUP, *tile), jnp.float32),
                pltpu.VMEM((RING, *tile), jnp.float32),
                pltpu.VMEM((6, RING * LANES, LANES), jnp.float32),
                pltpu.VMEM((32, RING * LANES), jnp.bfloat16),
                pltpu.VMEM(tile, jnp.float32),
                pltpu.VMEM((2, CHUNK, 2 * LANES), jnp.bfloat16),
                pltpu.VMEM((blocks, *tile), jnp.float32),
                pltpu.VMEM((GROUP, *tile), jnp.int32),
                pltpu.VMEM((blocks + 1, 32, 2 * LANES), jnp.float32),
                pltpu.VMEM((blocks, *tile), jnp.float32),
                pltpu.VMEM((GROUP, *tile), jnp.float32),
                pltpu.VMEM((GROUP, *tile), jnp.float32),
                dma((2,)), dma(()), dma(()), dma(()), dma((RING,)),
            ]
            + [dma(())] * 4,
            compiler_params=pltpu.CompilerParams(
                collective_id=which, has_side_effects=True, vmem_limit_bytes=40 << 20
            ),
            name=f"step_{blocks}",
        )

    listed = active.reshape(LANES, LANES)
    which, state = pl.pallas_call(
        functools.partial(prepare, grav),
        out_shape=(
            jax.ShapeDtypeStruct((1,), jnp.int32), jax.ShapeDtypeStruct((16, LANES), jnp.float32),
        ),
        in_specs=[pl.BlockSpec(memory_space=pltpu.VMEM)] * 4,
        out_specs=(
            pl.BlockSpec(memory_space=pltpu.SMEM), pl.BlockSpec(memory_space=pltpu.VMEM),
        ),
        name="prepare",
    )(listed, star_state, masses.reshape(1, LANES), levels.reshape(1, LANES))
    return lax.switch(
        which[0], [branch(i, b) for i, b in enumerate(BLOCK_COUNTS)], state, listed
    )


def solution(mesh):
    placed = (P(None, ("wide", "narrow")), P(("wide", "narrow")), P(("wide", "narrow")), P())
    return jax.shard_map(
        on_device,
        mesh=mesh,
        in_specs=placed,
        out_specs=P(None, ("wide", "narrow")),
        check_vma=False,
    )
```

```python
import functools

import jax
import jax.numpy as jnp
from jax import lax
from jax.experimental import pallas as pl
from jax.experimental.pallas import tpu as pltpu
from jax.sharding import PartitionSpec as P

MESH = pl.DeviceIdType.MESH
CAP = 96
LANES = 128
GROUP = 32
RING = 16
REACH = 4
CHUNK = 128
ROWS = 6
SOFT = 0.01
BLOCK_COUNTS = (10, 11, 12, 13, 14, 16, 20, 24)


def rows8(row):
    return jnp.broadcast_to(row, (8, LANES))


def lane_gather(tile, idx):
    return jnp.take_along_axis(tile, idx, axis=1, mode="promise_in_bounds")


def step_length(levels):
    return jnp.where(
        levels < 1.5,
        jnp.where(levels < 0.5, 1.0, 0.5),
        jnp.where(levels < 2.5, 0.25, 0.125),
    )


def halves(x):
    high = x.astype(jnp.bfloat16)
    return high, (x - high.astype(jnp.float32)).astype(jnp.bfloat16)


def strengths(targets, sources):
    sep = [sources[d] - targets[d] for d in range(3)]
    rel = [sources[3 + d] - targets[3 + d] for d in range(3)]
    dist_sq = (sep[0] * sep[0] + SOFT) + sep[1] * sep[1] + sep[2] * sep[2]
    inverse = lax.rsqrt(dist_sq)
    inverse_sq = inverse * inverse
    strength = inverse * inverse_sq
    radial = sep[0] * rel[0] + sep[1] * rel[1] + sep[2] * rel[2]
    turned = (radial * inverse_sq) * strength
    return [jnp.concatenate(pair, axis=1) for pair in zip(halves(strength), halves(turned))]


def kernel(
    blocks, state_hbm, active_hbm, out_ref, state, active_ref,
    old, tbuf, zbuf, spread, weigh, middle, pend, tgt, offs, accs, fresh, rout, rin,
    load, tsend, trecv, zsend, zrecv, fsend, frecv, rsend, rrecv,
):
    wide = lax.axis_index("wide")
    narrow = lax.axis_index("narrow")
    plane = wide // 4
    level = (wide % 4) * 4 + narrow // 2
    core = narrow % 2
    member = plane * 2 + core

    def device(plane, level, core):
        return (plane * 4 + level // 4, (level % 4) * 2 + core)

    def mate(i):
        other = (member + i) % GROUP
        return other, device(other // 2, level, other % 2)

    def along(shift):
        return device(plane, (level + shift + RING) % RING, core)

    barrier = pltpu.get_barrier_semaphore()

    def greet(i, carry):
        pl.semaphore_signal(barrier, inc=1, device_id=mate(i)[1], device_id_type=MESH)
        return carry

    quarter = level // 4
    odd = quarter % 2
    upper = level // 8
    inward = 1 - 2 * odd
    edge = level % 4 + odd * (3 - 2 * (level % 4))

    for k in range(1, REACH + 1):
        pl.semaphore_signal(barrier, inc=1, device_id=along(inward * k), device_id_type=MESH)

        @pl.when((edge >= k) | (upper == 0))
        def _():
            pl.semaphore_signal(barrier, inc=1, device_id=along(-inward * k), device_id_type=MESH)

    lax.fori_loop(1, GROUP, greet, 0)

    loads = [
        pltpu.make_async_copy(state_hbm, state, load.at[0]),
        pltpu.make_async_copy(active_hbm, active_ref, load.at[1]),
    ]
    for copy in loads:
        copy.start()
    for copy in loads:
        copy.wait()

    lane = lax.broadcasted_iota(jnp.int32, (8, LANES), 1)
    sub = lax.broadcasted_iota(jnp.int32, (8, LANES), 0)
    star = [state[d : d + 1, :] for d in range(12)]
    step = state[12:13, :]
    pred = []
    for d in range(3):
        x, v, a, j = star[d], star[3 + d], star[6 + d], star[9 + d]
        pred.append(x + step * (v + step * (a * 0.5 + step * j * (1.0 / 6.0))))
    for d in range(3):
        v, a, j = star[3 + d], star[6 + d], star[9 + d]
        pred.append(v + step * (a + step * j * 0.5))
    for d in range(6):
        zbuf[0, d : d + 1, :] = pred[d]
    zbuf[0, 6:7, :] = state[13:14, :]
    zbuf[0, 7:8, :] = jnp.zeros((1, LANES), jnp.float32)

    base = (wide * 8 + narrow) * LANES
    below = jnp.zeros((8, LANES), jnp.int32)
    through = jnp.zeros((8, LANES), jnp.int32)
    for v in range(16):
        entry = active_ref[8 * v : 8 * v + 8, :]
        below = below + jnp.where(entry < base, 1, 0)
        through = through + jnp.where(entry < base + LANES, 1, 0)

    def total(x):
        s = jnp.sum(x.astype(jnp.float32), axis=0, keepdims=True)
        s = jnp.sum(s, axis=1, keepdims=True)
        return jnp.broadcast_to(s, (8, LANES)).astype(jnp.int32)

    begin = total(below)
    count = total(through) - begin
    row_of = lax.shift_right_logical(begin + ((lane - begin) & (LANES - 1)), 7)
    found = jnp.zeros((8, LANES), jnp.int32)
    for v in range(16):
        entry = active_ref[8 * v : 8 * v + 8, :]
        found = found + jnp.where(row_of == sub + 8 * v, entry, 0)
    found = jnp.sum(found.astype(jnp.float32), axis=0, keepdims=True).astype(jnp.int32)
    picked = lane_gather(rows8(found), (lane + begin) & (LANES - 1)) - base
    picked = jnp.where(lane < count, picked, 0) & (LANES - 1)

    chosen = lane_gather(zbuf[0], picked)
    chosen = jnp.where(lane == LANES - 1, count.astype(jnp.float32), chosen)
    tbuf[member] = chosen

    pl.semaphore_wait(barrier, GROUP - 1 + REACH + edge + upper * (REACH - edge))

    def send_target(i, carry):
        pltpu.make_async_remote_copy(
            src_ref=tbuf.at[member, pl.ds(0, ROWS)], dst_ref=tbuf.at[member, pl.ds(0, ROWS)],
            send_sem=tsend, recv_sem=trecv, device_id=mate(i)[1], device_id_type=MESH,
        ).start()
        return carry

    def send_source(shift):
        slot = (RING - shift) % RING
        pltpu.make_async_remote_copy(
            src_ref=zbuf.at[0], dst_ref=zbuf.at[slot],
            send_sem=zsend, recv_sem=zrecv.at[slot], device_id=along(shift), device_id_type=MESH,
        ).start()

    def await_source(shift):
        slot = (RING + shift) % RING
        tile = zbuf.at[slot]
        pltpu.make_async_copy(tile, tile, zrecv.at[slot]).wait()

    for k in range(REACH, 0, -1):
        send_source(inward * k)

        @pl.when((edge >= k) | (upper == 1))
        def _():
            send_source(-inward * k)

    lax.fori_loop(1, GROUP, send_target, 0)

    old[0:8, :] = lane_gather(state[0:8, :], picked)
    old[8:16, :] = lane_gather(state[8:16, :], picked)

    mean = jnp.sum(zbuf[0], axis=1, keepdims=True) * (1.0 / LANES)
    middle[...] = jnp.where(sub < 6, jnp.broadcast_to(mean, (8, LANES)), 0.0)

    def spread_tile(slot, place):
        tile = zbuf[slot]
        turned = tile.T
        lanes = slice(place * LANES, (place + 1) * LANES)
        for d in range(6):
            spread[d, lanes, :] = jnp.broadcast_to(turned[:, d : d + 1], (LANES, LANES))
        mass = rows8(tile[6:7, :])
        rest = jnp.where(sub < 6, (tile - middle[...]) * mass, jnp.where(sub == 6, mass, 0.0))
        pieces = []
        for _ in range(3):
            pieces.append(rest.astype(jnp.bfloat16).astype(jnp.float32))
            rest = rest - pieces[-1]
        pieces.append(jnp.zeros((8, LANES), jnp.float32))
        weigh[:, lanes] = jnp.concatenate(pieces, axis=0).astype(jnp.bfloat16)

    spread_tile(0, 0)

    direct = zbuf.at[pl.ds(0, 2 * REACH)]
    passed = zbuf.at[pl.ds(0, RING - 1 - 2 * REACH)]

    def settle():
        for k in range(1, REACH + 1):
            await_source(-inward * k)

            @pl.when((edge < k) & (upper == 0))
            def _():
                send_source(-inward * k)

    def pass_up():
        pltpu.make_async_remote_copy(
            src_ref=zbuf.at[pl.ds(RING - REACH + 1, REACH - 1)],
            dst_ref=zbuf.at[pl.ds(RING - 2 * REACH + 1, REACH - 1)],
            send_sem=fsend, recv_sem=frecv, device_id=along(REACH), device_id_type=MESH,
        ).start()

    def pass_down():
        pltpu.make_async_remote_copy(
            src_ref=zbuf.at[pl.ds(1, REACH)], dst_ref=zbuf.at[pl.ds(1 + REACH, REACH)],
            send_sem=fsend, recv_sem=frecv, device_id=along(-REACH), device_id_type=MESH,
        ).start()

    others = tbuf.at[pl.ds(0, GROUP - 1), pl.ds(0, ROWS)]
    pltpu.make_async_copy(others, others, trecv).wait()

    def lay(k, carry):
        off, laid = carry[0], carry[1:]
        for u in range(8):
            o = k * 8 + u
            tile = tbuf[o]
            offs[o] = off
            rolled = lane_gather(tile, (lane - off) & (LANES - 1))
            laid = [jnp.where(lane + LANES * b >= off, rolled, laid[b]) for b in range(blocks)]
            off = off + rows8(
                jnp.broadcast_to(tile[0:1, LANES - 1 : LANES], (1, LANES))
            ).astype(jnp.int32)
        return (off, *laid)

    laid = lax.fori_loop(
        0, GROUP // 8, lay,
        (jnp.zeros((8, LANES), jnp.int32),) + (jnp.zeros((8, LANES), jnp.float32),) * blocks,
    )
    for b in range(blocks):
        tgt[b] = laid[1 + b]

    for k in range(1, REACH + 1):
        await_source(inward * k)

    @pl.when(quarter == 1)
    def _():
        settle()
        pass_up()
        pass_down()

    @pl.when(quarter == 2)
    def _():
        pass_down()

    @pl.when(quarter == 3)
    def _():
        pass_up()

    for k in range(1, REACH + 1):
        spread_tile((RING + inward * k) % RING, k)

    def work(first_tile, tiles):
        begin_row, end_row = first_tile * LANES, (first_tile + tiles) * LANES

        def product(lanes, piece):
            return jnp.dot(weigh[:, lanes], piece, preferred_element_type=jnp.float32)

        last = slice(end_row - CHUNK, end_row)

        def left():
            return product(last, pend[0]) + product(last, pend[1])

        def block(b, carry):
            targets = [
                jnp.broadcast_to(tgt[b, d : d + 1, :], (16, LANES)) for d in range(6)
            ]
            acc = jnp.zeros((32, 2 * LANES), jnp.float32)
            for first in range(begin_row, end_row, CHUNK):
                parts = [
                    strengths(targets, [spread[d, row : row + 16, :] for d in range(6)])
                    for row in range(first, first + CHUNK, 16)
                ]
                for p in range(2):
                    piece = jnp.concatenate([part[p] for part in parts], axis=0)
                    if True:
                        acc = acc + product(slice(first, first + CHUNK), piece)
                    else:
                        pend[p] = piece
            accs[b + 1] = accs[b + 1] + acc
            return carry

        lax.fori_loop(0, blocks, block, 0)

    accs[...] = jnp.zeros_like(accs)
    work(0, 1 + REACH)

    @pl.when(quarter == 0)
    def _():
        settle()
        pass_up()
        pass_down()

    @pl.when(quarter == 2)
    def _():
        settle()
        pass_up()

    @pl.when(quarter == 3)
    def _():
        settle()
        pass_down()

    for k in range(1, REACH + 1):
        spread_tile((RING - inward * k) % RING, REACH + k)
    work(1 + REACH, REACH)

    pltpu.make_async_copy(passed, passed, frecv).wait()
    for slot in range(REACH + 1, RING - REACH):
        spread_tile(slot, REACH + slot)
    work(1 + 2 * REACH, RING - 1 - 2 * REACH)

    for b in range(blocks):
        acc = accs[b + 1]
        acc = acc[0:8] + acc[8:16] + acc[16:24]
        drawn, dragged = acc[:, :LANES], acc[:, LANES:]
        here = tgt[b] - middle[...]
        pulled = drawn - here * rows8(drawn[6:7, :])
        slowed = dragged - here * rows8(dragged[6:7, :])
        fresh[b, 0:6, :] = pulled[0:6, :]
        fresh[b, 3:6, :] = pulled[3:6, :] - 3.0 * slowed[0:3, :]
        fresh[b, 6:8, :] = jnp.zeros((2, LANES), jnp.float32)

    def cut(o):
        off = offs[o]
        block_of = lax.shift_right_logical(off + ((lane - off) & (LANES - 1)), 7)
        mine = fresh[0]
        for b in range(1, blocks):
            mine = jnp.where(block_of == b, fresh[b], mine)
        return lane_gather(mine, (lane + off) & (LANES - 1))

    def give(first, count):
        cuts = [(mate(first + u), cut(mate(first + u)[0])) for u in range(count)]
        for (o, where), mine in cuts:
            rout[o] = mine
            pltpu.make_async_remote_copy(
                src_ref=rout.at[o, pl.ds(0, ROWS)], dst_ref=rin.at[member, pl.ds(0, ROWS)],
                send_sem=rsend, recv_sem=rrecv, device_id=where, device_id_type=MESH,
            ).start()

    def give8(k, carry):
        give(1 + 8 * k, 8)
        return carry

    lax.fori_loop(0, GROUP // 8 - 1, give8, 0)
    give(GROUP - 7, 7)
    rin[member] = cut(member)

    back = rin.at[pl.ds(0, GROUP - 1), pl.ds(0, ROWS)]
    pltpu.make_async_copy(back, back, rrecv).wait()
    sums = [rin[m] for m in range(8)]
    for m in range(8, GROUP):
        sums[m % 8] = sums[m % 8] + rin[m]
    while len(sums) > 1:
        sums = [sums[i] + sums[i + 1] for i in range(0, len(sums), 2)]
    new = sums[0]

    filled = lane[0:1, :] < count[0:1, :]
    step = old[12:13, :]
    half = step * 0.5
    twelfth = step * step * (1.0 / 12.0)
    for d in range(3):
        x0, v0 = old[d : d + 1, :], old[3 + d : 4 + d, :]
        a0, j0 = old[6 + d : 7 + d, :], old[9 + d : 10 + d, :]
        a1, j1 = new[d : d + 1, :], new[3 + d : 4 + d, :]
        v1 = v0 + half * (a0 + a1) + twelfth * (j0 - j1)
        x1 = x0 + half * (v0 + v1) + twelfth * (a0 - a1)
        for r, value in ((d, x1), (3 + d, v1), (6 + d, a1), (9 + d, j1)):
            out_ref[r : r + 1, :] = jnp.where(filled, value, 0.0)[:, :CAP]

    pltpu.make_async_copy(others, others, tsend).wait()
    pltpu.make_async_copy(direct, direct, zsend).wait()
    pltpu.make_async_copy(passed, passed, fsend).wait()
    pltpu.make_async_copy(back, back, rsend).wait()


def prepare(grav, active_ref, star_ref, mass_ref, level_ref, which_ref, state_ref):
    state_ref[0:12, :] = star_ref[...]
    state_ref[12:13, :] = step_length(level_ref[...].astype(jnp.float32))
    state_ref[13:14, :] = mass_ref[...] * grav
    state_ref[14:16, :] = jnp.zeros((2, LANES), jnp.float32)

    counts = [jnp.zeros((8, LANES), jnp.int32) for _ in range(RING)]
    for v in range(16):
        plane = lax.shift_right_logical(active_ref[8 * v : 8 * v + 8, :], 8) & (RING - 1)
        counts = [c + jnp.where(plane == g, 1, 0) for g, c in enumerate(counts)]
    rows = [jnp.sum(c.astype(jnp.float32), axis=0, keepdims=True) for c in counts]
    most = jnp.max(jnp.sum(jnp.concatenate(rows, axis=0), axis=1, keepdims=True))
    which_ref[0] = sum(jnp.where(most > b * LANES, 1, 0) for b in BLOCK_COUNTS[:-1])


def on_device(star_state, masses, levels, active):
    local_count = star_state.shape[1]
    owners = lax.axis_size(("wide", "narrow"))
    grav = 1.0 / (local_count * owners)
    tile = (8, LANES)
    dma = pltpu.SemaphoreType.DMA

    def branch(which, blocks):
        return pl.pallas_call(
            functools.partial(kernel, blocks),
            out_shape=jax.ShapeDtypeStruct((12, CAP), jnp.float32),
            in_specs=[pl.BlockSpec(memory_space=pl.ANY)] * 2,
            out_specs=pl.BlockSpec(memory_space=pltpu.VMEM),
            scratch_shapes=[
                pltpu.VMEM((16, LANES), jnp.float32),
                pltpu.VMEM((LANES, LANES), jnp.int32),
                pltpu.VMEM((16, LANES), jnp.float32),
                pltpu.VMEM((GROUP, *tile), jnp.float32),
                pltpu.VMEM((RING, *tile), jnp.float32),
                pltpu.VMEM((6, RING * LANES, LANES), jnp.float32),
                pltpu.VMEM((32, RING * LANES), jnp.bfloat16),
                pltpu.VMEM(tile, jnp.float32),
                pltpu.VMEM((2, CHUNK, 2 * LANES), jnp.bfloat16),
                pltpu.VMEM((blocks, *tile), jnp.float32),
                pltpu.VMEM((GROUP, *tile), jnp.int32),
                pltpu.VMEM((blocks + 1, 32, 2 * LANES), jnp.float32),
                pltpu.VMEM((blocks, *tile), jnp.float32),
                pltpu.VMEM((GROUP, *tile), jnp.float32),
                pltpu.VMEM((GROUP, *tile), jnp.float32),
                dma((2,)), dma(()), dma(()), dma(()), dma((RING,)),
            ]
            + [dma(())] * 4,
            compiler_params=pltpu.CompilerParams(
                collective_id=which, has_side_effects=True, vmem_limit_bytes=40 << 20
            ),
            name=f"step_{blocks}",
        )

    listed = active.reshape(LANES, LANES)
    which, state = pl.pallas_call(
        functools.partial(prepare, grav),
        out_shape=(
            jax.ShapeDtypeStruct((1,), jnp.int32), jax.ShapeDtypeStruct((16, LANES), jnp.float32),
        ),
        in_specs=[pl.BlockSpec(memory_space=pltpu.VMEM)] * 4,
        out_specs=(
            pl.BlockSpec(memory_space=pltpu.SMEM), pl.BlockSpec(memory_space=pltpu.VMEM),
        ),
        name="prepare",
    )(listed, star_state, masses.reshape(1, LANES), levels.reshape(1, LANES))
    return lax.switch(
        which[0], [branch(i, b) for i, b in enumerate(BLOCK_COUNTS)], state, listed
    )


def solution(mesh):
    placed = (P(None, ("wide", "narrow")), P(("wide", "narrow")), P(("wide", "narrow")), P())
    return jax.shard_map(
        on_device,
        mesh=mesh,
        in_specs=placed,
        out_specs=P(None, ("wide", "narrow")),
        check_vma=False,
    )
```
